256 devices in a mesh: fsdp: 16 (over x_lo, y, core), group: 8 (over z), dp: 2 (over x_hi).
Axes of the slice: x: 4 (x_hi: 2, x_lo: 2; x = x_hi * 2 + x_lo), y: 4, z: 8, core: 2. Of those that a mesh axis runs over, the one named last changes fastest.
Arguments:
- hidden_states: bfloat16 [32, 16, 256, 5120], P(('fsdp', 'dp'), 'group'), may hold values from -6 to 6
- kv_weight: bfloat16 [5120, 1024], P('fsdp'), may hold values from -0.078125 to 0.078125
- sensitivity: bfloat16 [32, 16, 256, 1024], P(('fsdp', 'dp'), 'group'), may hold values from -6 to 6
- logp_shift: float32 [32, 16, 256], P(('fsdp', 'dp'), 'group'), may hold values from -0.6 to 0.6
- token_mask: int32 [32, 16, 256], P(('fsdp', 'dp'), 'group'), may hold values 0 or 1
- lengths: int32 [32, 16], P(('fsdp', 'dp'), 'group'), may hold values from 64 to 256
- rewards: int32 [32, 16], P(('fsdp', 'dp'), 'group'), may hold values from 0 to 100
Outputs:
- kv_grad: float32 [5120, 1024], P('fsdp', 'group')
The draws below stay inside these ranges and needn't reach their ends.
All inputs are finite; a program needn't handle non-finite values. No bound on the sum of `token_mask` on one device may be relied on, other than what follows from the above.
Results may differ from the reference program's by a relative error of at most 0.0029.
Values may be sent and summed in bfloat16 or wider, within the bound.
No kernel may reach another device: no remote copies, remote signals or barrier semaphores. Data moves between devices by JAX's collectives and lax.ppermute only.
A program may use at most 128 MiB of HBM per device.

```python
import math
import jax
import jax.numpy as jnp
from jax import lax

D = 5120
GROUP_SIZE = 16
LEN = 256
KV = 1024
PROMPTS = 32


def draw_lengths(key, part):
    key = jax.random.fold_in(key, 11)
    first_key, second_key = jax.random.split(key)
    slots_total = PROMPTS * GROUP_SIZE
    sampled = jax.random.randint(first_key, (slots_total,), LEN // 4, LEN + 1)
    chosen_slot = jax.random.randint(second_key, (), 0, slots_total)
    sampled = jnp.where(jnp.arange(slots_total) == chosen_slot, LEN, sampled)
    return sampled.reshape(PROMPTS, GROUP_SIZE).astype(jnp.int32)


def draw_rewards(key, part):
    key = jax.random.fold_in(key, 23)
    keys = jax.random.split(key, 8)
    spread_vals = jax.random.randint(keys[0], (PROMPTS, GROUP_SIZE), 0, 101)
    kinds = jax.random.randint(keys[1], (PROMPTS,), 0, 16)
    tied_prompt = jax.random.randint(keys[2], (), 0, PROMPTS)
    open_prompt = (tied_prompt + 1 + jax.random.randint(keys[3], (), 0, PROMPTS - 1)) % PROMPTS
    prompt_ids = jnp.arange(PROMPTS)
    kinds = jnp.where(prompt_ids == tied_prompt, 1, kinds)
    kinds = jnp.where(prompt_ids == open_prompt, 15, kinds)
    base_vals = jax.random.randint(keys[4], (PROMPTS, 1), 0, 100)
    odd_slot = jax.random.randint(keys[5], (PROMPTS, 1), 0, GROUP_SIZE)
    slot_ids = jnp.arange(GROUP_SIZE)[None, :]
    near_equal = base_vals + (slot_ids == odd_slot).astype(jnp.int32)
    all_equal = jnp.broadcast_to(base_vals, (PROMPTS, GROUP_SIZE))
    lowest_slot = jax.random.randint(keys[6], (), 0, GROUP_SIZE)
    highest_slot = (lowest_slot + 1 + jax.random.randint(keys[7], (), 0, GROUP_SIZE - 1)) % GROUP_SIZE
    with_ends = jnp.where(slot_ids == lowest_slot, 0, jnp.where(slot_ids == highest_slot, 100, spread_vals))
    spread_vals = jnp.where((prompt_ids == open_prompt)[:, None], with_ends, spread_vals)
    chosen = jnp.where(kinds[:, None] == 0, all_equal, jnp.where(kinds[:, None] == 1, near_equal, spread_vals))
    return chosen.astype(jnp.int32)


def plant(array, stream_key, least, top_value):
    longest = array.shape.index(max(array.shape))
    spots = []
    for shift in (0, 1):
        where = [jax.random.randint(jax.random.fold_in(stream_key, axis), (), 0, length) for axis, length in enumerate(array.shape)]
        where[longest] = (where[longest] + shift) % array.shape[longest]
        spots.append(tuple(where))
    return array.at[spots[0]].set(least).at[spots[1]].set(top_value)


def block_scale(own_key, shape, cuts, low, largest):
    def one(dim, shards_of):
        draws = jax.random.uniform(jax.random.fold_in(jax.random.fold_in(own_key, 6), dim), (shards_of,), jnp.float32, low / len(cuts), largest / len(cuts))
        return jnp.repeat(jnp.exp(draws), shape[dim] // shards_of).reshape((-1,) + (1,) * (len(shape) - dim - 1))

    level = one(*cuts[0])
    for cut in cuts[1:]:
        level = level * one(*cut)
    return level


def bell_draw(rng, shape, scale, reach, cuts=(), held_as=jnp.bfloat16):
    values = jax.random.normal(rng, shape, jnp.float32) * scale
    if len(cuts) > 0:
        values = block_scale(rng, shape, cuts, -0.22, 0.18) * values
    return jnp.clip(values, min=-reach, max=reach).astype(held_as)


def setup_inputs(seed: int = 0) -> dict:
    key_list = jax.random.split(jax.random.key(seed), 8)
    return {
        "hidden_states": bell_draw(key_list[0], (PROMPTS, GROUP_SIZE, LEN, D), 1.0, 6.0, ((0, 32), (1, 8))),
        "kv_weight": bell_draw(key_list[1], (D, KV), D ** -0.5, 0.078125, ((0, 16),)),
        "sensitivity": bell_draw(key_list[2], (PROMPTS, GROUP_SIZE, LEN, KV), 1.0, 6.0, ((0, 32), (1, 8))),
        "logp_shift": bell_draw(key_list[3], (PROMPTS, GROUP_SIZE, LEN), 0.1, 0.6, ((0, 32), (1, 8)), jnp.float32),
        "token_mask": plant((jax.random.randint(key_list[4], (PROMPTS, GROUP_SIZE, LEN), 0, 8) < 7).astype(jnp.int32), jax.random.fold_in(key_list[4], 1), 0, 1),
        "lengths": draw_lengths(jax.random.fold_in(key_list[7], 71), 0),
        "rewards": draw_rewards(jax.random.fold_in(key_list[7], 71), 0),
    }


CLIP_LOW = 0.8
CLIP_HIGH = 1.28
LOSS_SCALE = 64.0

def reference(hidden_states, kv_weight, sensitivity, logp_shift, token_mask, lengths, rewards):
    scale_read = 0.3 / math.sqrt(KV)
    reward_vals = rewards.astype(jnp.float32)
    reward_mean = lax.optimization_barrier(jnp.sum(reward_vals, axis=1)) / GROUP_SIZE
    squares = lax.optimization_barrier(jnp.sum(reward_vals * reward_vals, axis=1))
    spread = jnp.sqrt(jnp.maximum(squares / GROUP_SIZE - reward_mean * reward_mean, 0.0))
    advantage = (reward_vals - reward_mean[:, None]) / jnp.maximum(spread, 1.0)[:, None]
    positions = jnp.arange(LEN, dtype=jnp.int32)
    kept = ((positions[None, None, :] < lengths[:, :, None]) & (token_mask == 1)).astype(jnp.float32)
    coef = -LOSS_SCALE * advantage[:, :, None] * kept / lengths[:, :, None].astype(jnp.float32)

    def one_prompt(running, items):
        states, sens_block, shift_block, coef_block = items
        token_rows = states.reshape(-1, D)
        sens_rows = sens_block.reshape(-1, KV)
        projected = jnp.dot(token_rows, kv_weight, preferred_element_type=jnp.float32)
        linear = scale_read * lax.optimization_barrier(jnp.sum(projected * sens_rows.astype(jnp.float32), axis=1))
        ratios = jnp.exp(shift_block.reshape(-1) + linear)
        factor = jnp.clip(ratios, CLIP_LOW, CLIP_HIGH) * coef_block.reshape(-1) * scale_read
        step_dir = (factor[:, None] * sens_rows.astype(jnp.float32)).astype(jnp.bfloat16)
        update = lax.dot_general(token_rows, step_dir, (((0,), (0,)), ((), ())), preferred_element_type=jnp.float32)
        return (running + update, None)
    start_grad = jnp.zeros((D, KV), jnp.float32)
    kv_grad, unused = lax.scan(one_prompt, start_grad, (hidden_states, sensitivity, logp_shift, coef))
    return kv_grad
```

```python
import math

import jax
import jax.numpy as jnp
from jax import lax
from jax.sharding import PartitionSpec as P

GROUP_SIZE = 16
CLIP_LOW = 0.8
CLIP_HIGH = 1.28
LOSS_SCALE = 64.0

NX, NY, NC, NZ, NDP = 2, 4, 2, 8, 2
PLANE = [(x, y, c) for x in range(NX) for y in range(NY) for c in range(NC)]


def place(x, y, c):
    return (x * NY + y % NY) * NC + c


def ring_x(x, y, c, dp, hop):
    ring = (dp * NX + x + hop) % (NX * NDP)
    return place(ring % NX, y, c) * NDP + ring // NX


OTHER_CORE = [(place(x, y, c), place(x, y, 1 - c)) for x, y, c in PLANE]


def to_core(a):
    return lax.ppermute(a, "fsdp", OTHER_CORE)


def to_y(a, hop):
    return lax.ppermute(a, "fsdp", [(place(x, y, c), place(x, y + hop, c)) for x, y, c in PLANE])


def to_x(a, hop):
    pairs = [
        (place(x, y, c) * NDP + dp, ring_x(x, y, c, dp, hop)) for x, y, c in PLANE for dp in range(NDP)
    ]
    return lax.ppermute(a, ("fsdp", "dp"), pairs)


def to_z(a, hop):
    return lax.ppermute(a, "group", [(z, (z + hop) % NZ) for z in range(NZ)])


def to_z_xor(a, bit):
    return lax.ppermute(a, "group", [(z, z ^ bit) for z in range(NZ)])


def to_dp(a):
    return lax.ppermute(a, "dp", [(0, 1), (1, 0)])


def shards(hidden_states, kv_weight, sensitivity, logp_shift, token_mask, lengths, rewards):
    seq_slots = hidden_states.shape[2]
    width = hidden_states.shape[3]
    columns = kv_weight.shape[1]
    rows_own = kv_weight.shape[0]
    rows = rows_own * NC
    half = columns // NC
    piece = half // 2
    scale_read = 0.3 / math.sqrt(columns)
    at = lax.axis_index("fsdp")
    core = at % NC
    y = (at // NC) % NY
    x = at // (NC * NY)
    f32, bf16 = jnp.float32, jnp.bfloat16

    def my_columns(a):
        return lax.dynamic_slice_in_dim(a, core * half, half, axis=1)

    def its_columns(a):
        return lax.dynamic_slice_in_dim(a, (1 - core) * half, half, axis=1)

    w_mine = my_columns(kv_weight)
    w_theirs = to_core(its_columns(kv_weight))
    first = core == 0
    chip_rows = jnp.concatenate(
        [jnp.where(first, w_mine, w_theirs), jnp.where(first, w_theirs, w_mine)], axis=0
    )
    w = {}
    w[0, 0, 0], w[0, 0, 1] = chip_rows[:, :piece], chip_rows[:, piece:]
    w[0, 1, 0] = to_y(w[0, 0, 0], -1)
    w[0, 3, 0] = to_y(w[0, 0, 0], 1)
    w[1, 0, 0] = to_x(w[0, 0, 0], -1)
    w[1, 0, 1] = to_x(w[0, 0, 1], 1)
    w[0, 1, 1] = to_y(w[0, 0, 1], -1)
    w[0, 3, 1] = to_y(w[0, 0, 1], 1)
    w[1, 1, 0] = to_x(w[0, 1, 0], -1)
    w[1, 3, 0] = to_x(w[0, 3, 0], 1)
    w[0, 2, 0] = to_y(w[0, 1, 0], -1)
    w[0, 2, 1] = to_y(w[0, 3, 1], 1)
    w[1, 1, 1] = to_x(w[0, 1, 1], -1)
    w[1, 3, 1] = to_x(w[0, 3, 1], 1)
    w[1, 2, 0] = to_x(w[0, 2, 0], -1)
    w[1, 2, 1] = to_x(w[0, 2, 1], 1)

    hid_mine = hidden_states.reshape(-1, width)
    hid_theirs = to_core(hid_mine)
    sens_all = sensitivity.reshape(-1, columns)
    sens = jnp.concatenate([my_columns(sens_all), to_core(its_columns(sens_all))], axis=0)

    reward_vals = rewards.astype(f32)
    sums = jnp.concatenate(
        [jnp.sum(reward_vals, axis=1), jnp.sum(reward_vals * reward_vals, axis=1)]
    )
    for bit in (1, 2, 4):
        sums = sums + to_z_xor(sums, bit)
    reward_mean = sums[0] / GROUP_SIZE
    spread = jnp.sqrt(jnp.maximum(sums[1] / GROUP_SIZE - reward_mean * reward_mean, 0.0))
    advantage = (reward_vals - reward_mean) / jnp.maximum(spread, 1.0)
    positions = lax.broadcasted_iota(jnp.int32, (1, 1, seq_slots), 2)
    kept = ((positions < lengths[:, :, None]) & (token_mask == 1)).astype(f32)
    coef = -LOSS_SCALE * advantage[:, :, None] * kept / lengths[:, :, None].astype(f32)
    per_token = jnp.stack([logp_shift.reshape(-1), coef.reshape(-1)])
    per_token = jnp.concatenate([per_token, to_core(per_token)], axis=1)

    hid = {}
    for dx in range(NX):
        for dy in range(NY):
            start = ((x ^ dx) * NY + (y + dy) % NY) * rows
            hid[dx, dy] = jnp.concatenate(
                [lax.dynamic_slice_in_dim(a, start, rows, axis=1) for a in (hid_mine, hid_theirs)], axis=0
            )
    hid_keys = list(hid)
    hid = dict(zip(hid_keys, lax.optimization_barrier([hid[k] for k in hid_keys])))

    read = None
    for key in w:
        dx, dy, p = key
        part = jnp.dot(hid[dx, dy], w[key], preferred_element_type=f32)
        term = jnp.sum(part * sens[:, p * piece : (p + 1) * piece].astype(f32), axis=1)
        read = term if read is None else read + term
    tokens = hid_mine.shape[0]
    read_theirs = to_core(read)
    read = read + jnp.concatenate([read_theirs[tokens:], read_theirs[:tokens]])
    ratios = jnp.exp(per_token[0] + scale_read * read)
    factor = jnp.clip(ratios, CLIP_LOW, CLIP_HIGH) * per_token[1] * scale_read
    step_dir = (factor[:, None] * sens.astype(f32)).astype(bf16)
    steps = (step_dir[:, :piece], step_dir[:, piece:])

    def term(dx, dy, p, *received):
        out = lax.dot_general(
            hid[dx, dy], steps[p], (((0,), (0,)), ((), ())), preferred_element_type=f32
        )
        for r in received:
            out = out + r.astype(f32)
        return out

    def narrow(*args):
        return term(*args).astype(bf16)

    r020 = to_x(narrow(1, 2, 0), 1)
    r021 = to_x(narrow(1, 2, 1), -1)
    r011 = to_x(narrow(1, 1, 1), 1)
    r031 = to_x(narrow(1, 3, 1), -1)
    s010 = to_y(narrow(0, 2, 0, r020), 1)
    s031 = to_y(narrow(0, 2, 1, r021), -1)
    r010 = to_x(narrow(1, 1, 0), 1)
    r030 = to_x(narrow(1, 3, 0), -1)
    t001 = to_y(narrow(0, 1, 1, r011), 1)
    u001 = to_y(narrow(0, 3, 1, r031, s031), -1)
    v000 = to_x(narrow(1, 0, 0), 1)
    v001 = to_x(narrow(1, 0, 1), -1)
    t000 = to_y(narrow(0, 1, 0, r010, s010), 1)
    u000 = to_y(narrow(0, 3, 0, r030), -1)
    chip_sum = jnp.concatenate(
        [term(0, 0, 0, t000, u000, v000), term(0, 0, 1, t001, u001, v001)], axis=1
    )

    keep = lax.dynamic_slice_in_dim(chip_sum, core * rows_own, rows_own, axis=0)
    give = lax.dynamic_slice_in_dim(chip_sum, (1 - core) * rows_own, rows_own, axis=0)
    got = to_core(give)
    row_block = jnp.concatenate([jnp.where(first, keep, got), jnp.where(first, got, keep)], axis=1)

    own = columns // NZ
    z = lax.axis_index("group")
    total = lax.dynamic_slice_in_dim(row_block, z * own, own, axis=1)
    narrow_block = row_block.astype(bf16)
    for hop in (4, 3, 5, 2, 6, 1, 7):
        block = lax.dynamic_slice_in_dim(narrow_block, ((z + hop) % NZ) * own, own, axis=1)
        total = total + to_z(block, hop).astype(f32)
    return total + to_dp(total)


def solution(mesh):
    in_specs = (
        P(("fsdp", "dp"), "group", None, None),
        P("fsdp", None),
        P(("fsdp", "dp"), "group", None, None),
        P(("fsdp", "dp"), "group", None),
        P(("fsdp", "dp"), "group", None),
        P(("fsdp", "dp"), "group"),
        P(("fsdp", "dp"), "group"),
    )
    out_specs = P("fsdp", "group")
    return jax.shard_map(shards, mesh=mesh, in_specs=in_specs, out_specs=out_specs, check_vma=False)
```

```python
import functools
import math

import jax
import jax.numpy as jnp
from jax import lax
from jax.experimental import pallas as pl
from jax.experimental.pallas import tpu as pltpu
from jax.sharding import PartitionSpec as P

GROUP_SIZE = 16
CLIP_LOW = 0.8
CLIP_HIGH = 1.28
LOSS_SCALE = 64.0

NX, NY, NC, NZ, NDP = 2, 4, 2, 8, 2
PLANE = [(x, y, c) for x in range(NX) for y in range(NY) for c in range(NC)]


def place(x, y, c):
    return (x * NY + y % NY) * NC + c


def ring_x(x, y, c, dp, hop):
    ring = (dp * NX + x + hop) % (NX * NDP)
    return place(ring % NX, y, c) * NDP + ring // NX


OTHER_CORE = [(place(x, y, c), place(x, y, 1 - c)) for x, y, c in PLANE]


def to_core(a):
    return lax.ppermute(a, "fsdp", OTHER_CORE)


def along_y(a, way):
    pairs = [(place(x, y, c), place(x, y + (way if c == 0 else -way), c)) for x, y, c in PLANE]
    return lax.ppermute(a, "fsdp", pairs)


def rows_along_y(a, way):
    pairs = []
    for x, y, c in PLANE:
        for z in range(NZ):
            owner = (c + z) % NC
            far_y = y + (1 if c == 0 else -1)
            ends = place(x, y, c) * NZ + z, place(x, far_y, owner) * NZ + z
            pairs.append(ends if way > 0 else ends[::-1])
    return lax.ppermute(a, ("fsdp", "group"), pairs)


def along_z(a):
    pairs = []
    for x, y, c in PLANE:
        for z in range(NZ):
            to = z ^ 1 if c == 0 else (z + (1 if z % 2 else -1)) % NZ
            pairs.append((place(x, y, c) * NZ + z, place(x, y, c) * NZ + to))
    return lax.ppermute(a, ("fsdp", "group"), pairs)


def along_x(a, way):
    pairs = [
        (place(x, y, c) * NDP + dp, ring_x(x, y, c, dp, way if c == 0 else -way))
        for x, y, c in PLANE
        for dp in range(NDP)
    ]
    return lax.ppermute(a, ("fsdp", "dp"), pairs)


def to_z_xor(a, bit):
    return lax.ppermute(a, "group", [(z, z ^ bit) for z in range(NZ)])


def to_z(a, hop):
    return lax.ppermute(a, "group", [(z, (z + hop) % NZ) for z in range(NZ)])


def to_dp(a):
    return lax.ppermute(a, "dp", [(0, 1), (1, 0)])


def after(a, earlier):
    return lax.optimization_barrier((a, earlier))[0]


def after(a, earlier):
    return lax.optimization_barrier((a, earlier))[0]


def read_kernel(count, spots, mine, theirs, sens_mine, sens_theirs, *refs):
    blocks, (before, after_, *hids), (padded, sems) = refs[:count], refs[count : count + 2 + count], refs[-2:]
    rows = blocks[0].shape[0]
    window = hids[0].shape[1]
    spare = window - rows
    tokens = mine.shape[0]
    copies = []
    for i in range(count):
        start = pl.multiple_of(spots[2 * i] * 128, 128)
        offset = pl.multiple_of(spots[2 * i + 1] * spare, spare)
        padded[i, :spare] = jnp.zeros((spare, padded.shape[2]), padded.dtype)
        padded[i, rows:] = jnp.zeros((spare, padded.shape[2]), padded.dtype)
        moves = (
            (blocks[i], padded.at[i, pl.ds(offset, rows)]),
            (mine.at[:, pl.ds(start, window)], hids[i].at[pl.ds(0, tokens)]),
            (theirs.at[:, pl.ds(start, window)], hids[i].at[pl.ds(tokens, tokens)]),
        )
        copies.append([pltpu.make_async_copy(src, dst, sems.at[i, j]) for j, (src, dst) in enumerate(moves)])
        for copy in copies[-1]:
            copy.start()
    after_[...] = before[...]
    chunk = 256
    for i in range(count):
        for copy in copies[i]:
            copy.wait()
        for at in range(0, 2 * tokens, chunk):
            sens = sens_mine if at < tokens else sens_theirs
            part = jnp.dot(hids[i][at : at + chunk], padded[i], preferred_element_type=jnp.float32)
            part = part * sens[at % tokens : at % tokens + chunk].astype(jnp.float32)
            total = after_[at : at + chunk]
            for lane in range(0, part.shape[1], 128):
                total = total + part[:, lane : lane + 128]
            after_[at : at + chunk] = total


def read_blocks(spots, mine, theirs, sens_mine, sens_theirs, blocks, before):
    count = len(blocks)
    rows, columns = blocks[0].shape
    window = -(-rows // 128) * 128
    tokens = 2 * mine.shape[0]
    vmem = pl.BlockSpec(memory_space=pltpu.VMEM)
    whole = pl.BlockSpec(memory_space=pl.ANY)
    hid = jax.ShapeDtypeStruct((tokens, window), mine.dtype)
    return pl.pallas_call(
        functools.partial(read_kernel, count),
        in_specs=[pl.BlockSpec(memory_space=pltpu.SMEM), whole, whole, vmem, vmem] + [whole] * count + [vmem],
        out_specs=[vmem] * (1 + count),
        out_shape=[jax.ShapeDtypeStruct((tokens, 128), jnp.float32)] + [hid] * count,
        scratch_shapes=[
            pltpu.VMEM((count, window, columns), mine.dtype),
            pltpu.SemaphoreType.DMA((count, 3)),
        ],
        cost_estimate=pl.CostEstimate(flops=0, bytes_accessed=0, transcendentals=0),
        compiler_params=pltpu.CompilerParams(vmem_limit_bytes=32 * 2**20),
    )(spots, mine, theirs, sens_mine, sens_theirs, *blocks, before)


def shards(hidden_states, kv_weight, sensitivity, logp_shift, token_mask, lengths, rewards):
    seq_slots = hidden_states.shape[2]
    width = hidden_states.shape[3]
    columns = kv_weight.shape[1]
    rows = kv_weight.shape[0]
    scale_read = 0.3 / math.sqrt(columns)
    at = lax.axis_index("fsdp")
    core = at % NC
    y = (at // NC) % NY
    x = at // (NC * NY)
    first = core == 0
    f32, bf16 = jnp.float32, jnp.bfloat16

    hid_mine = hidden_states.reshape(-1, width)
    hid_theirs = to_core(hid_mine)
    sens_mine = sensitivity.reshape(-1, columns)
    sens_theirs = to_core(sens_mine)
    sens = jnp.concatenate([sens_mine, sens_theirs], axis=0)
    positions = lax.broadcasted_iota(jnp.int32, (1, 1, seq_slots), 2)
    kept = ((positions < lengths[:, :, None]) & (token_mask == 1)).astype(f32)
    spread_out = lambda a: jnp.broadcast_to(a.astype(f32)[:, :, None], kept.shape).reshape(-1)
    per_token = jnp.stack([logp_shift.reshape(-1), kept.reshape(-1), spread_out(lengths), spread_out(rewards)])
    tokens = per_token.shape[1]
    token_theirs = to_core(per_token)

    kind = (core + lax.axis_index("group")) % NC
    next_y = jnp.where(first, 1, NY - 1)
    spots = {
        "own": (0, 0, core),
        "side": (1, 0, core),
        "near": (0, next_y, kind),
        "near_other": (0, next_y, 1 - kind),
        "near_side": (1, next_y, kind),
        "near_side_other": (1, next_y, 1 - kind),
        "far": (0, 2, kind),
        "far_side": (1, 2, kind),
    }
    h, w = {}, {"own": kv_weight}

    def read_terms(before, *names):
        where = []
        for name in names:
            dx, dy, owner = spots[name]
            chip = (x ^ dx) * NY + (y + dy) % NY
            where += [chip * (NC * rows // 128) + owner * (rows // 128), owner]
        total, *cut = read_blocks(
            jnp.stack(where).astype(jnp.int32), hid_mine, hid_theirs, sens_mine, sens_theirs,
            [w[name] for name in names], before,
        )
        h.update(zip(names, cut))
        return total

    w["near"] = rows_along_y(kv_weight, -1)
    w["side"] = along_x(kv_weight, -1)
    per_token = jnp.concatenate([per_token, token_theirs], axis=1)
    shift, kept, lens, reward_vals = per_token
    reward_pairs = reward_vals.reshape(NC, -1, seq_slots)[:, :, 0]
    sums = jnp.concatenate([jnp.sum(reward_pairs, axis=1), jnp.sum(reward_pairs * reward_pairs, axis=1)])
    sums = sums + to_z_xor(sums, 1)

    near, _, sums = lax.optimization_barrier((w["near"], w["side"], sums))
    w["near_other"] = along_z(near)
    w["near_side"] = along_x(near, -1)
    w["far"] = along_y(near, -1)
    sums = sums + to_z_xor(sums, 2)
    read = read_terms(jnp.zeros((2 * tokens, 128), f32), "own", "side", "near")

    near_side, far, _, sums, read = lax.optimization_barrier(
        (w["near_side"], w["far"], w["near_other"], sums, read)
    )
    w["near_side_other"] = along_z(near_side)
    w["far_side"] = along_x(far, -1)
    sums = sums + to_z_xor(sums, 4)
    reward_mean = sums[:NC] / GROUP_SIZE
    spread = jnp.sqrt(jnp.maximum(sums[NC:] / GROUP_SIZE - reward_mean * reward_mean, 0.0))
    advantage = (reward_vals.reshape(NC, -1) - reward_mean[:, None]) / jnp.maximum(spread, 1.0)[:, None]
    coef = -LOSS_SCALE * advantage.reshape(-1) * kept / lens
    read = read_terms(read, "near_other", "near_side", "far")
    coef, read = lax.optimization_barrier((coef, read))
    read = jnp.sum(read_terms(read, "near_side_other", "far_side"), axis=1)

    read_theirs = to_core(read)
    read = read + jnp.concatenate([read_theirs[tokens:], read_theirs[:tokens]])
    ratios = jnp.exp(shift + scale_read * read)
    factor = jnp.clip(ratios, CLIP_LOW, CLIP_HIGH) * coef * scale_read
    step_dir = (factor[:, None] * sens.astype(f32)).astype(bf16)

    def term(name, step):
        out = lax.dot_general(h[name], step, (((0,), (0,)), ((), ())), preferred_element_type=f32)
        return name, lax.optimization_barrier(out)

    def add(named, *received):
        name, total = named
        spare = total.shape[0] - rows
        total = jnp.where(spots[name][2] == 0, total[:rows], total[spare:])
        for r in received:
            total = total + r.astype(f32)
        return total

    far_side = along_x(add(term("far_side", step_dir)).astype(bf16), 1)
    near_side_other = along_z(add(term("near_side_other", step_dir)).astype(bf16))
    far = term("far", step_dir)
    near_side = term("near_side", step_dir)
    near_other = add(term("near_other", step_dir)).astype(bf16)

    step, near_other = lax.optimization_barrier((step_dir, near_other, far_side, near_side_other))[:2]
    far = along_y(add(far, far_side).astype(bf16), 1)
    near_side = along_x(add(near_side, near_side_other).astype(bf16), 1)
    near_other = along_z(near_other)
    near = term("near", step)
    side = add(term("side", step)).astype(bf16)

    step, side = lax.optimization_barrier((step_dir, side, far, near_side, near_other))[:2]
    near = rows_along_y(add(near, near_side, far, near_other).astype(bf16), 1)
    side = along_x(side, 1)
    row_block = add(term("own", step), side, near)

    own = columns // NZ
    z = lax.axis_index("group")
    total = lax.dynamic_slice_in_dim(row_block, z * own, own, axis=1)
    narrow_block = row_block.astype(bf16)
    for hop in (4, 3, 5, 2, 6, 1, 7):
        block = lax.dynamic_slice_in_dim(narrow_block, ((z + hop) % NZ) * own, own, axis=1)
        total = total + to_z(block, hop).astype(f32)
    return total + to_dp(total)


def solution(mesh):
    in_specs = (
        P(("fsdp", "dp"), "group", None, None),
        P("fsdp", None),
        P(("fsdp", "dp"), "group", None, None),
        P(("fsdp", "dp"), "group", None),
        P(("fsdp", "dp"), "group", None),
        P(("fsdp", "dp"), "group"),
        P(("fsdp", "dp"), "group"),
    )
    out_specs = P("fsdp", "group")
    return jax.shard_map(shards, mesh=mesh, in_specs=in_specs, out_specs=out_specs, check_vma=False)
```

```python
import functools
import math

import jax
import jax.numpy as jnp
from jax import lax
from jax.experimental import pallas as pl
from jax.experimental.pallas import tpu as pltpu
from jax.sharding import PartitionSpec as P

GROUP_SIZE = 16
CLIP_LOW = 0.8
CLIP_HIGH = 1.28
LOSS_SCALE = 64.0
VMEM_GRANT = 16 * 2**20

NX, NY, NC, NZ, NDP = 2, 4, 2, 8, 2
PLANE = [(x, y, c) for x in range(NX) for y in range(NY) for c in range(NC)]


def place(x, y, c):
    return (x * NY + y % NY) * NC + c


def ring_x(x, y, c, dp, hop):
    ring = (dp * NX + x + hop) % (NX * NDP)
    return place(ring % NX, y, c) * NDP + ring // NX


OTHER_CORE = [(place(x, y, c), place(x, y, 1 - c)) for x, y, c in PLANE]


def to_core(a):
    return lax.ppermute(a, "fsdp", OTHER_CORE)


def along_y(a, way):
    pairs = [(place(x, y, c), place(x, y + (way if c == 0 else -way), c)) for x, y, c in PLANE]
    return lax.ppermute(a, "fsdp", pairs)


def rows_along_y(a, way):
    pairs = []
    for x, y, c in PLANE:
        for z in range(NZ):
            owner = (c + z) % NC
            far_y = y + (1 if c == 0 else -1)
            ends = place(x, y, c) * NZ + z, place(x, far_y, owner) * NZ + z
            pairs.append(ends if way > 0 else ends[::-1])
    return lax.ppermute(a, ("fsdp", "group"), pairs)


def along_z(a):
    pairs = []
    for x, y, c in PLANE:
        for z in range(NZ):
            to = z ^ 1 if c == 0 else (z + (1 if z % 2 else -1)) % NZ
            pairs.append((place(x, y, c) * NZ + z, place(x, y, c) * NZ + to))
    return lax.ppermute(a, ("fsdp", "group"), pairs)


def along_x(a, way):
    pairs = [
        (place(x, y, c) * NDP + dp, ring_x(x, y, c, dp, way if c == 0 else -way))
        for x, y, c in PLANE
        for dp in range(NDP)
    ]
    return lax.ppermute(a, ("fsdp", "dp"), pairs)


def to_z_xor(a, bit):
    return lax.ppermute(a, "group", [(z, z ^ bit) for z in range(NZ)])


def to_z(a, hop):
    return lax.ppermute(a, "group", [(z, (z + hop) % NZ) for z in range(NZ)])


def to_dp(a):
    return lax.ppermute(a, "dp", [(0, 1), (1, 0)])


def after(a, earlier):
    return lax.optimization_barrier((a, earlier))[0]


def after(a, earlier):
    return lax.optimization_barrier((a, earlier))[0]


def owner_of(kind):
    core = lax.axis_index("fsdp") % NC
    if kind == "core":
        return core
    planar = (core + lax.axis_index("group")) % NC
    return planar if kind == "plane" else 1 - planar


def read_kernel(first, kinds, sens_mine, sens_theirs, *refs):
    count = len(kinds)
    blocks, hids, refs = refs[:count], refs[count : 2 * count], refs[2 * count :]
    owners = [owner_of(kind) for kind in kinds]
    before, refs = (None, refs) if first else (refs[0], refs[1:])
    total_ref, padded = refs
    rows = blocks[0].shape[0]
    spare = padded.shape[1] - rows
    tokens = sens_mine.shape[0]
    chunk = 256
    for i in range(count):
        padded[i, :spare] = jnp.zeros((spare, padded.shape[2]), padded.dtype)
        padded[i, rows:] = jnp.zeros((spare, padded.shape[2]), padded.dtype)
        padded[i, pl.ds(pl.multiple_of(owners[i] * spare, spare), rows)] = blocks[i][...]
        for at in range(0, 2 * tokens, chunk):
            sens = sens_mine if at < tokens else sens_theirs
            part = jnp.dot(hids[i][at : at + chunk], padded[i], preferred_element_type=jnp.float32)
            part = part * sens[at % tokens : at % tokens + chunk].astype(jnp.float32)
            lanes = [part[:, lane : lane + 128] for lane in range(0, part.shape[1], 128)]
            if i > 0:
                lanes.append(total_ref[at : at + chunk])
            elif not first:
                lanes.append(before[at : at + chunk])
            total_ref[at : at + chunk] = sum(lanes[1:], lanes[0])


def read_blocks(kinds, sens, blocks, hids, before, flops=0):
    vmem = pl.BlockSpec(memory_space=pltpu.VMEM)
    count = len(blocks)
    tokens, window = hids[0].shape
    earlier = [] if before is None else [before]
    return pl.pallas_call(
        functools.partial(read_kernel, before is None, kinds),
        in_specs=[vmem] * (2 + 2 * count + len(earlier)),
        out_specs=vmem,
        out_shape=jax.ShapeDtypeStruct((tokens, 128), jnp.float32),
        scratch_shapes=[pltpu.VMEM((count, window, blocks[0].shape[1]), hids[0].dtype)],
        cost_estimate=pl.CostEstimate(flops=flops, bytes_accessed=0, transcendentals=0),
        compiler_params=pltpu.CompilerParams(vmem_limit_bytes=VMEM_GRANT),
    )(*sens, *blocks, *hids, *earlier)


def shards(hidden_states, kv_weight, sensitivity, logp_shift, token_mask, lengths, rewards):
    seq_slots = hidden_states.shape[2]
    width = hidden_states.shape[3]
    columns = kv_weight.shape[1]
    rows = kv_weight.shape[0]
    scale_read = 0.3 / math.sqrt(columns)
    at = lax.axis_index("fsdp")
    core = at % NC
    y = (at // NC) % NY
    x = at // (NC * NY)
    first = core == 0
    f32, bf16 = jnp.float32, jnp.bfloat16

    hid_mine = hidden_states.reshape(-1, width)
    hid_theirs = to_core(hid_mine)
    tokens = hid_mine.shape[0]
    sens_mine = sensitivity.reshape(-1, columns)
    sens_theirs = to_core(sens_mine)

    next_y = jnp.where(first, 1, NY - 1)
    spots = {
        "own": (0, 0, "core"),
        "side": (1, 0, "core"),
        "near": (0, next_y, "plane"),
        "near_other": (0, next_y, "passed"),
        "near_side": (1, next_y, "plane"),
        "near_side_other": (1, next_y, "passed"),
        "far": (0, 2, "plane"),
        "far_side": (1, 2, "plane"),
    }
    window = -(-rows // 128) * 128
    spare = window - rows
    h, w = {}, {"own": kv_weight}

    def windows(*names):
        cut = []
        for name in names:
            dx, dy, owner = spots[name]
            start = ((x ^ dx) * NY + (y + dy) % NY) * NC * rows + owner_of(owner) * (rows - spare)
            both = [lax.dynamic_slice_in_dim(a, start, window, axis=1) for a in (hid_mine, hid_theirs)]
            cut.append(jnp.concatenate(both, axis=0))
        h.update(zip(names, lax.optimization_barrier(tuple(cut))))

    def read_terms(before, *names):
        return read_blocks(
            [spots[name][2] for name in names], (sens_mine, sens_theirs), [w[name] for name in names], [h[name] for name in names], before
        )

    w["near"] = rows_along_y(kv_weight, -1)
    w["side"] = along_x(kv_weight, -1)
    reward_vals = rewards.astype(f32)
    both = jnp.concatenate([reward_vals, reward_vals * reward_vals])
    sums = jnp.broadcast_to(jnp.sum(both, axis=1)[:, None, None], (2, reward_vals.shape[1], seq_slots))
    for bit in (1, 2):
        sums = sums + to_z_xor(sums, bit)

    near, w["side"], sums = lax.optimization_barrier((w["near"], w["side"], sums))
    w["near"] = near
    w["near_other"] = along_z(near)
    w["near_side"] = along_x(near, -1)
    w["far"] = along_y(near, -1)
    windows("own", "side")
    sums, h["own"] = lax.optimization_barrier((sums, h["own"]))
    sums = sums + to_z_xor(sums, 4)
    read = read_terms(None, "own", "side")

    near_side, far, _, read = lax.optimization_barrier((w["near_side"], w["far"], w["near_other"], read))
    w["near_side_other"] = along_z(near_side)
    w["far_side"] = along_x(far, -1)
    sums, read = lax.optimization_barrier((sums, read))
    reward_mean = sums[0] / GROUP_SIZE
    spread = jnp.sqrt(jnp.maximum(sums[1] / GROUP_SIZE - reward_mean * reward_mean, 0.0))
    advantage = (reward_vals[:, :, None] - reward_mean) / jnp.maximum(spread, 1.0)
    positions = lax.broadcasted_iota(jnp.int32, (1, 1, seq_slots), 2)
    kept = ((positions < lengths[:, :, None]) & (token_mask == 1)).astype(f32)
    coef = -LOSS_SCALE * advantage * kept / lengths[:, :, None].astype(f32)
    per_token = jnp.stack([logp_shift.reshape(-1), coef.reshape(-1)])
    windows("near", "near_other", "near_side", "far")
    read = read_terms(read, "near", "near_other", "near_side", "far")
    windows("near_side_other", "far_side")
    read = read_terms(read, "near_side_other", "far_side")
    read, per_token = lax.optimization_barrier((jnp.sum(read, axis=1), per_token))
    shift, coef = jnp.concatenate([per_token, to_core(per_token)], axis=1)

    read_theirs = to_core(read)
    read = read + jnp.concatenate([read_theirs[tokens:], read_theirs[:tokens]])
    ratios = jnp.exp(shift + scale_read * read)
    factor = jnp.clip(ratios, CLIP_LOW, CLIP_HIGH) * coef * scale_read
    sens = jnp.concatenate([sens_mine, sens_theirs], axis=0)
    step_dir = (factor[:, None] * sens.astype(f32)).astype(bf16)

    def term(name, step):
        out = lax.dot_general(h[name], step, (((0,), (0,)), ((), ())), preferred_element_type=f32)
        return name, lax.optimization_barrier(out)

    def add(named, *received):
        name, total = named
        spare = total.shape[0] - rows
        total = jnp.where(owner_of(spots[name][2]) == 0, total[:rows], total[spare:])
        for r in received:
            total = total + r.astype(f32)
        return total

    far_side = along_x(add(term("far_side", step_dir)).astype(bf16), 1)
    near_side_other = along_z(add(term("near_side_other", step_dir)).astype(bf16))
    far = term("far", step_dir)
    near_side = term("near_side", step_dir)
    near_other = add(term("near_other", step_dir)).astype(bf16)

    step, near_other = lax.optimization_barrier((step_dir, near_other, far_side, near_side_other))[:2]
    far = along_y(add(far, far_side).astype(bf16), 1)
    near_side = along_x(add(near_side, near_side_other).astype(bf16), 1)
    near_other = along_z(near_other)
    near = term("near", step)
    side = add(term("side", step)).astype(bf16)

    step, side = lax.optimization_barrier((step_dir, side, far, near_side, near_other))[:2]
    near = rows_along_y(add(near, near_side, far, near_other).astype(bf16), 1)
    side = along_x(side, 1)
    row_block = add(term("own", step), side, near)

    own = columns // NZ
    z = lax.axis_index("group")
    total = lax.dynamic_slice_in_dim(row_block, z * own, own, axis=1)
    narrow_block = row_block.astype(bf16)
    for hop in (7, 1, 6, 2, 5, 3, 4):
        block = lax.dynamic_slice_in_dim(narrow_block, ((z + hop) % NZ) * own, own, axis=1)
        total = total + to_z(block, hop).astype(f32)
    return total + to_dp(total)


def solution(mesh):
    in_specs = (
        P(("fsdp", "dp"), "group", None, None),
        P("fsdp", None),
        P(("fsdp", "dp"), "group", None, None),
        P(("fsdp", "dp"), "group", None),
        P(("fsdp", "dp"), "group", None),
        P(("fsdp", "dp"), "group"),
        P(("fsdp", "dp"), "group"),
    )
    out_specs = P("fsdp", "group")
    return jax.shard_map(shards, mesh=mesh, in_specs=in_specs, out_specs=out_specs, check_vma=False)
```

```python
import functools
import math

import jax
import jax.numpy as jnp
from jax import lax
from jax.experimental import pallas as pl
from jax.experimental.pallas import tpu as pltpu
from jax.sharding import PartitionSpec as P

GROUP_SIZE = 16
CLIP_LOW = 0.8
CLIP_HIGH = 1.28
LOSS_SCALE = 64.0
VMEM_GRANT = 16 * 2**20

NX, NY, NC, NZ, NDP = 2, 4, 2, 8, 2
PLANE = [(x, y, c) for x in range(NX) for y in range(NY) for c in range(NC)]


def place(x, y, c):
    return (x * NY + y % NY) * NC + c


def ring_x(x, y, c, dp, hop):
    ring = (dp * NX + x + hop) % (NX * NDP)
    return place(ring % NX, y, c) * NDP + ring // NX


OTHER_CORE = [(place(x, y, c), place(x, y, 1 - c)) for x, y, c in PLANE]


def to_core(a):
    return lax.ppermute(a, "fsdp", OTHER_CORE)


def along_y(a, way):
    pairs = [(place(x, y, c), place(x, y + (way if c == 0 else -way), c)) for x, y, c in PLANE]
    return lax.ppermute(a, "fsdp", pairs)


def rows_along_y(a, way):
    pairs = []
    for x, y, c in PLANE:
        for z in range(NZ):
            owner = (c + z) % NC
            far_y = y + (1 if c == 0 else -1)
            ends = place(x, y, c) * NZ + z, place(x, far_y, owner) * NZ + z
            pairs.append(ends if way > 0 else ends[::-1])
    return lax.ppermute(a, ("fsdp", "group"), pairs)


def along_z(a):
    pairs = []
    for x, y, c in PLANE:
        for z in range(NZ):
            to = z ^ 1 if c == 0 else (z + (1 if z % 2 else -1)) % NZ
            pairs.append((place(x, y, c) * NZ + z, place(x, y, c) * NZ + to))
    return lax.ppermute(a, ("fsdp", "group"), pairs)


def along_x(a, way):
    pairs = [
        (place(x, y, c) * NDP + dp, ring_x(x, y, c, dp, way if c == 0 else -way))
        for x, y, c in PLANE
        for dp in range(NDP)
    ]
    return lax.ppermute(a, ("fsdp", "dp"), pairs)


def to_z_xor(a, bit):
    return lax.ppermute(a, "group", [(z, z ^ bit) for z in range(NZ)])


def to_dp(a):
    return lax.ppermute(a, "dp", [(0, 1), (1, 0)])


def after(a, earlier):
    return lax.optimization_barrier((a, earlier))[0]


def after(a, earlier):
    return lax.optimization_barrier((a, earlier))[0]


def owner_of(kind):
    core = lax.axis_index("fsdp") % NC
    if kind == "core":
        return core
    planar = (core + lax.axis_index("group")) % NC
    return planar if kind == "plane" else 1 - planar


def read_kernel(first, kinds, sens_mine, sens_theirs, *refs):
    count = len(kinds)
    blocks, hids, refs = refs[:count], refs[count : 2 * count], refs[2 * count :]
    owners = [owner_of(kind) for kind in kinds]
    before, refs = (None, refs) if first else (refs[0], refs[1:])
    total_ref, padded = refs
    rows = blocks[0].shape[0]
    spare = padded.shape[1] - rows
    tokens = sens_mine.shape[0]
    chunk = 256
    for i in range(count):
        padded[i, :spare] = jnp.zeros((spare, padded.shape[2]), padded.dtype)
        padded[i, rows:] = jnp.zeros((spare, padded.shape[2]), padded.dtype)
        padded[i, pl.ds(pl.multiple_of(owners[i] * spare, spare), rows)] = blocks[i][...]
        for at in range(0, 2 * tokens, chunk):
            sens = sens_mine if at < tokens else sens_theirs
            part = jnp.dot(hids[i][at : at + chunk], padded[i], preferred_element_type=jnp.float32)
            part = part * sens[at % tokens : at % tokens + chunk].astype(jnp.float32)
            lanes = [part[:, lane : lane + 128] for lane in range(0, part.shape[1], 128)]
            if i > 0:
                lanes.append(total_ref[at : at + chunk])
            elif not first:
                lanes.append(before[at : at + chunk])
            total_ref[at : at + chunk] = sum(lanes[1:], lanes[0])


def read_blocks(kinds, sens, blocks, hids, before, flops=0):
    vmem = pl.BlockSpec(memory_space=pltpu.VMEM)
    count = len(blocks)
    tokens, window = hids[0].shape
    earlier = [] if before is None else [before]
    return pl.pallas_call(
        functools.partial(read_kernel, before is None, kinds),
        in_specs=[vmem] * (2 + 2 * count + len(earlier)),
        out_specs=vmem,
        out_shape=jax.ShapeDtypeStruct((tokens, 128), jnp.float32),
        scratch_shapes=[pltpu.VMEM((count, window, blocks[0].shape[1]), hids[0].dtype)],
        cost_estimate=pl.CostEstimate(flops=flops, bytes_accessed=0, transcendentals=0),
        compiler_params=pltpu.CompilerParams(vmem_limit_bytes=VMEM_GRANT),
    )(*sens, *blocks, *hids, *earlier)


def shards(hidden_states, kv_weight, sensitivity, logp_shift, token_mask, lengths, rewards):
    seq_slots = hidden_states.shape[2]
    width = hidden_states.shape[3]
    columns = kv_weight.shape[1]
    rows = kv_weight.shape[0]
    scale_read = 0.3 / math.sqrt(columns)
    at = lax.axis_index("fsdp")
    core = at % NC
    y = (at // NC) % NY
    x = at // (NC * NY)
    first = core == 0
    f32, bf16 = jnp.float32, jnp.bfloat16

    hid_mine = hidden_states.reshape(-1, width)
    hid_theirs = to_core(hid_mine)
    tokens = hid_mine.shape[0]
    sens_mine = sensitivity.reshape(-1, columns)
    sens_theirs = to_core(sens_mine)

    next_y = jnp.where(first, 1, NY - 1)
    spots = {
        "own": (0, 0, "core"),
        "side": (1, 0, "core"),
        "near": (0, next_y, "plane"),
        "near_other": (0, next_y, "passed"),
        "near_side": (1, next_y, "plane"),
        "near_side_other": (1, next_y, "passed"),
        "far": (0, 2, "plane"),
        "far_side": (1, 2, "plane"),
    }
    window = -(-rows // 128) * 128
    spare = window - rows
    h, w = {}, {"own": kv_weight}

    def windows(*names):
        cut = []
        for name in names:
            dx, dy, owner = spots[name]
            start = ((x ^ dx) * NY + (y + dy) % NY) * NC * rows + owner_of(owner) * (rows - spare)
            both = [lax.dynamic_slice_in_dim(a, start, window, axis=1) for a in (hid_mine, hid_theirs)]
            cut.append(jnp.concatenate(both, axis=0))
        h.update(zip(names, lax.optimization_barrier(tuple(cut))))

    def read_terms(before, *names):
        return read_blocks(
            [spots[name][2] for name in names], (sens_mine, sens_theirs), [w[name] for name in names], [h[name] for name in names], before
        )

    w["near"] = rows_along_y(kv_weight, -1)
    w["side"] = along_x(kv_weight, -1)
    reward_vals = rewards.astype(f32)
    both = jnp.concatenate([reward_vals, reward_vals * reward_vals])
    sums = jnp.broadcast_to(jnp.sum(both, axis=1)[:, None, None], (2, reward_vals.shape[1], seq_slots))
    for bit in (1, 2):
        sums = sums + to_z_xor(sums, bit)

    near, w["side"], sums = lax.optimization_barrier((w["near"], w["side"], sums))
    w["near"] = near
    w["near_other"] = along_z(near)
    w["near_side"] = along_x(near, -1)
    w["far"] = along_y(near, -1)
    windows("own", "side")
    sums, h["own"] = lax.optimization_barrier((sums, h["own"]))
    sums = sums + to_z_xor(sums, 4)
    read = read_terms(None, "own", "side")

    near_side, far, _, read = lax.optimization_barrier((w["near_side"], w["far"], w["near_other"], read))
    w["near_side_other"] = along_z(near_side)
    w["far_side"] = along_x(far, -1)
    sums, read = lax.optimization_barrier((sums, read))
    reward_mean = sums[0] / GROUP_SIZE
    spread = jnp.sqrt(jnp.maximum(sums[1] / GROUP_SIZE - reward_mean * reward_mean, 0.0))
    advantage = (reward_vals[:, :, None] - reward_mean) / jnp.maximum(spread, 1.0)
    positions = lax.broadcasted_iota(jnp.int32, (1, 1, seq_slots), 2)
    kept = ((positions < lengths[:, :, None]) & (token_mask == 1)).astype(f32)
    coef = -LOSS_SCALE * advantage * kept / lengths[:, :, None].astype(f32)
    per_token = jnp.stack([logp_shift.reshape(-1), coef.reshape(-1)])
    windows("near", "near_other", "near_side", "far")
    read = read_terms(read, "near", "near_other", "near_side", "far")
    windows("near_side_other", "far_side")
    read = read_terms(read, "near_side_other", "far_side")
    read, per_token = lax.optimization_barrier((jnp.sum(read, axis=1), per_token))
    shift, coef = jnp.concatenate([per_token, to_core(per_token)], axis=1)

    read_theirs = to_core(read)
    read = read + jnp.concatenate([read_theirs[tokens:], read_theirs[:tokens]])
    ratios = jnp.exp(shift + scale_read * read)
    factor = jnp.clip(ratios, CLIP_LOW, CLIP_HIGH) * coef * scale_read
    sens = jnp.concatenate([sens_mine, sens_theirs], axis=0)
    step_dir = (factor[:, None] * sens.astype(f32)).astype(bf16)

    def term(name, step):
        out = lax.dot_general(h[name], step, (((0,), (0,)), ((), ())), preferred_element_type=f32)
        return name, lax.optimization_barrier(out)

    def add(named, *received):
        name, total = named
        spare = total.shape[0] - rows
        total = jnp.where(owner_of(spots[name][2]) == 0, total[:rows], total[spare:])
        for r in received:
            total = total + r.astype(f32)
        return total

    far_side = along_x(add(term("far_side", step_dir)).astype(bf16), 1)
    near_side_other = along_z(add(term("near_side_other", step_dir)).astype(bf16))
    far = term("far", step_dir)
    near_side = term("near_side", step_dir)
    near_other = add(term("near_other", step_dir)).astype(bf16)

    step, near_other = lax.optimization_barrier((step_dir, near_other, far_side, near_side_other))[:2]
    far = along_y(add(far, far_side).astype(bf16), 1)
    near_side = along_x(add(near_side, near_side_other).astype(bf16), 1)
    near_other = along_z(near_other)
    near = term("near", step)
    side = add(term("side", step)).astype(bf16)

    step, side = lax.optimization_barrier((step_dir, side, far, near_side, near_other))[:2]
    near = rows_along_y(add(near, near_side, far, near_other).astype(bf16), 1)
    side = along_x(side, 1)
    row_block = add(term("own", step), side, near)

    own = columns // NZ
    blocks = row_block.astype(bf16).reshape(rows, NZ, own).transpose(1, 0, 2)
    blocks = lax.all_to_all(blocks, "group", 0, 0)
    z = lax.axis_index("group")
    others = lax.broadcasted_iota(jnp.int32, (NZ, 1, 1), 0) != z
    total = jnp.sum(jnp.where(others, blocks.astype(f32), 0.0), axis=0)
    total = total + lax.dynamic_slice_in_dim(row_block, z * own, own, axis=1)
    return total + to_dp(total)


def solution(mesh):
    in_specs = (
        P(("fsdp", "dp"), "group", None, None),
        P("fsdp", None),
        P(("fsdp", "dp"), "group", None, None),
        P(("fsdp", "dp"), "group", None),
        P(("fsdp", "dp"), "group", None),
        P(("fsdp", "dp"), "group"),
        P(("fsdp", "dp"), "group"),
    )
    out_specs = P("fsdp", "group")
    return jax.shard_map(shards, mesh=mesh, in_specs=in_specs, out_specs=out_specs, check_vma=False)
```

```python
import functools
import math

import jax
import jax.numpy as jnp
from jax import lax
from jax.experimental import pallas as pl
from jax.experimental.pallas import tpu as pltpu
from jax.sharding import PartitionSpec as P

GROUP_SIZE = 16
CLIP_LOW = 0.8
CLIP_HIGH = 1.28
LOSS_SCALE = 64.0
VMEM_GRANT = 16 * 2**20

NX, NY, NC, NZ, NDP = 2, 4, 2, 8, 2
PLANE = [(x, y, c) for x in range(NX) for y in range(NY) for c in range(NC)]


def place(x, y, c):
    return (x * NY + y % NY) * NC + c


def ring_x(x, y, c, dp, hop):
    ring = (dp * NX + x + hop) % (NX * NDP)
    return place(ring % NX, y, c) * NDP + ring // NX


OTHER_CORE = [(place(x, y, c), place(x, y, 1 - c)) for x, y, c in PLANE]


def to_core(a):
    return lax.ppermute(a, "fsdp", OTHER_CORE)


def along_y(a, way):
    pairs = [(place(x, y, c), place(x, y + (way if c == 0 else -way), c)) for x, y, c in PLANE]
    return lax.ppermute(a, "fsdp", pairs)


def rows_along_y(a, way):
    pairs = []
    for x, y, c in PLANE:
        for z in range(NZ):
            owner = (c + z) % NC
            far_y = y + (1 if c == 0 else -1)
            ends = place(x, y, c) * NZ + z, place(x, far_y, owner) * NZ + z
            pairs.append(ends if way > 0 else ends[::-1])
    return lax.ppermute(a, ("fsdp", "group"), pairs)


def along_z(a):
    pairs = []
    for x, y, c in PLANE:
        for z in range(NZ):
            to = z ^ 1 if c == 0 else (z + (1 if z % 2 else -1)) % NZ
            pairs.append((place(x, y, c) * NZ + z, place(x, y, c) * NZ + to))
    return lax.ppermute(a, ("fsdp", "group"), pairs)


def along_x(a, way):
    pairs = [
        (place(x, y, c) * NDP + dp, ring_x(x, y, c, dp, way if c == 0 else -way))
        for x, y, c in PLANE
        for dp in range(NDP)
    ]
    return lax.ppermute(a, ("fsdp", "dp"), pairs)


def to_z_xor(a, bit):
    return lax.ppermute(a, "group", [(z, z ^ bit) for z in range(NZ)])


def to_dp(a):
    return lax.ppermute(a, "dp", [(0, 1), (1, 0)])


def after(a, earlier):
    return lax.optimization_barrier((a, earlier))[0]


def after(a, earlier):
    return lax.optimization_barrier((a, earlier))[0]


def owner_of(kind):
    core = lax.axis_index("fsdp") % NC
    if kind == "core":
        return core
    planar = (core + lax.axis_index("group")) % NC
    return planar if kind == "plane" else 1 - planar


def read_kernel(first, kinds, sens_mine, sens_theirs, *refs):
    count = len(kinds)
    blocks, hids, refs = refs[:count], refs[count : 2 * count], refs[2 * count :]
    owners = [owner_of(kind) for kind in kinds]
    before, refs = (None, refs) if first else (refs[0], refs[1:])
    total_ref, padded = refs
    rows = blocks[0].shape[0]
    spare = padded.shape[1] - rows
    tokens = sens_mine.shape[0]
    chunk = 256
    for i in range(count):
        padded[i, :spare] = jnp.zeros((spare, padded.shape[2]), padded.dtype)
        padded[i, rows:] = jnp.zeros((spare, padded.shape[2]), padded.dtype)
        padded[i, pl.ds(pl.multiple_of(owners[i] * spare, spare), rows)] = blocks[i][...]
        for at in range(0, 2 * tokens, chunk):
            sens = sens_mine if at < tokens else sens_theirs
            part = jnp.dot(hids[i][at : at + chunk], padded[i], preferred_element_type=jnp.float32)
            part = part * sens[at % tokens : at % tokens + chunk].astype(jnp.float32)
            lanes = [part[:, lane : lane + 128] for lane in range(0, part.shape[1], 128)]
            if i > 0:
                lanes.append(total_ref[at : at + chunk])
            elif not first:
                lanes.append(before[at : at + chunk])
            total_ref[at : at + chunk] = sum(lanes[1:], lanes[0])


def read_blocks(kinds, sens, blocks, hids, before, flops=0):
    vmem = pl.BlockSpec(memory_space=pltpu.VMEM)
    count = len(blocks)
    tokens, window = hids[0].shape
    earlier = [] if before is None else [before]
    return pl.pallas_call(
        functools.partial(read_kernel, before is None, kinds),
        in_specs=[vmem] * (2 + 2 * count + len(earlier)),
        out_specs=vmem,
        out_shape=jax.ShapeDtypeStruct((tokens, 128), jnp.float32),
        scratch_shapes=[pltpu.VMEM((count, window, blocks[0].shape[1]), hids[0].dtype)],
        cost_estimate=pl.CostEstimate(flops=flops, bytes_accessed=0, transcendentals=0),
        compiler_params=pltpu.CompilerParams(vmem_limit_bytes=VMEM_GRANT),
    )(*sens, *blocks, *hids, *earlier)


def shards(hidden_states, kv_weight, sensitivity, logp_shift, token_mask, lengths, rewards):
    seq_slots = hidden_states.shape[2]
    width = hidden_states.shape[3]
    columns = kv_weight.shape[1]
    rows = kv_weight.shape[0]
    scale_read = 0.3 / math.sqrt(columns)
    at = lax.axis_index("fsdp")
    core = at % NC
    y = (at // NC) % NY
    x = at // (NC * NY)
    first = core == 0
    f32, bf16 = jnp.float32, jnp.bfloat16

    hid_mine = hidden_states.reshape(-1, width)
    hid_theirs = to_core(hid_mine)
    tokens = hid_mine.shape[0]
    sens_mine = sensitivity.reshape(-1, columns)
    sens_theirs = to_core(sens_mine)

    next_y = jnp.where(first, 1, NY - 1)
    spots = {
        "own": (0, 0, "core"),
        "side": (1, 0, "core"),
        "near": (0, next_y, "plane"),
        "near_other": (0, next_y, "passed"),
        "near_side": (1, next_y, "plane"),
        "near_side_other": (1, next_y, "passed"),
        "far": (0, 2, "plane"),
        "far_side": (1, 2, "plane"),
    }
    window = -(-rows // 128) * 128
    spare = window - rows
    h, w = {}, {"own": kv_weight}

    def windows(*names):
        cut = []
        for name in names:
            dx, dy, owner = spots[name]
            start = ((x ^ dx) * NY + (y + dy) % NY) * NC * rows + owner_of(owner) * (rows - spare)
            both = [lax.dynamic_slice_in_dim(a, start, window, axis=1) for a in (hid_mine, hid_theirs)]
            cut.append(jnp.concatenate(both, axis=0))
        h.update(zip(names, lax.optimization_barrier(tuple(cut))))

    def read_terms(before, *names):
        return read_blocks(
            [spots[name][2] for name in names], (sens_mine, sens_theirs), [w[name] for name in names], [h[name] for name in names], before
        )

    w["near"] = rows_along_y(kv_weight, -1)
    w["side"] = along_x(kv_weight, -1)
    reward_vals = rewards.astype(f32)
    both = jnp.concatenate([reward_vals, reward_vals * reward_vals])
    sums = jnp.broadcast_to(jnp.sum(both, axis=1)[:, None, None], (2, reward_vals.shape[1], seq_slots))
    for bit in (1, 2):
        sums = sums + to_z_xor(sums, bit)

    near, w["side"], sums = lax.optimization_barrier((w["near"], w["side"], sums))
    w["near"] = near
    w["near_other"] = along_z(near)
    w["near_side"] = along_x(near, -1)
    w["far"] = along_y(near, -1)
    windows("own", "side")
    sums, h["own"] = lax.optimization_barrier((sums, h["own"]))
    sums = sums + to_z_xor(sums, 4)
    read = read_terms(None, "own", "side")

    near_side, far, _, read = lax.optimization_barrier((w["near_side"], w["far"], w["near_other"], read))
    w["near_side_other"] = along_z(near_side)
    w["far_side"] = along_x(far, -1)
    sums, read = lax.optimization_barrier((sums, read))
    reward_mean = sums[0] / GROUP_SIZE
    spread = jnp.sqrt(jnp.maximum(sums[1] / GROUP_SIZE - reward_mean * reward_mean, 0.0))
    advantage = (reward_vals[:, :, None] - reward_mean) / jnp.maximum(spread, 1.0)
    positions = lax.broadcasted_iota(jnp.int32, (1, 1, seq_slots), 2)
    kept = ((positions < lengths[:, :, None]) & (token_mask == 1)).astype(f32)
    coef = -LOSS_SCALE * advantage * kept / lengths[:, :, None].astype(f32)
    per_token = jnp.stack([logp_shift.reshape(-1), coef.reshape(-1)])
    windows("near", "near_other", "near_side", "far")
    read = read_terms(read, "near", "near_other", "near_side", "far")
    windows("near_side_other", "far_side")
    read = read_terms(read, "near_side_other", "far_side")
    read, per_token = lax.optimization_barrier((jnp.sum(read, axis=1), per_token))
    shift, coef = jnp.concatenate([per_token, to_core(per_token)], axis=1)

    read_theirs = to_core(read)
    read = read + jnp.concatenate([read_theirs[tokens:], read_theirs[:tokens]])
    ratios = jnp.exp(shift + scale_read * read)
    factor = jnp.clip(ratios, CLIP_LOW, CLIP_HIGH) * coef * scale_read
    sens = jnp.concatenate([sens_mine, sens_theirs], axis=0)
    step_dir = (factor[:, None] * sens.astype(f32)).astype(bf16)

    def term(name, step):
        out = lax.dot_general(h[name], step, (((0,), (0,)), ((), ())), preferred_element_type=f32)
        return name, lax.optimization_barrier(out)

    def add(named, *received):
        name, total = named
        spare = total.shape[0] - rows
        total = jnp.where(owner_of(spots[name][2]) == 0, total[:rows], total[spare:])
        for r in received:
            total = total + r.astype(f32)
        return total

    far_side = along_x(add(term("far_side", step_dir)).astype(bf16), 1)
    near_side_other = along_z(add(term("near_side_other", step_dir)).astype(bf16))
    far = term("far", step_dir)
    near_side = term("near_side", step_dir)
    near_other = add(term("near_other", step_dir)).astype(bf16)

    step, near_other = lax.optimization_barrier((step_dir, near_other, far_side, near_side_other))[:2]
    far = along_y(add(far, far_side).astype(bf16), 1)
    near_side = along_x(add(near_side, near_side_other).astype(bf16), 1)
    near_other = along_z(near_other)
    near = term("near", step)
    side = add(term("side", step)).astype(bf16)

    step, side = lax.optimization_barrier((step_dir, side, far, near_side, near_other))[:2]
    near = rows_along_y(add(near, near_side, far, near_other).astype(bf16), 1)
    side = along_x(side, 1)
    row_block = add(term("own", step), side, near)

    own = columns // NZ
    blocks = row_block.astype(bf16).reshape(rows, NZ, own).transpose(1, 0, 2)
    blocks = lax.all_to_all(blocks, "group", 0, 0)
    total = jnp.sum(blocks.astype(f32), axis=0)
    return total + to_dp(total)


def solution(mesh):
    in_specs = (
        P(("fsdp", "dp"), "group", None, None),
        P("fsdp", None),
        P(("fsdp", "dp"), "group", None, None),
        P(("fsdp", "dp"), "group", None),
        P(("fsdp", "dp"), "group", None),
        P(("fsdp", "dp"), "group"),
        P(("fsdp", "dp"), "group"),
    )
    out_specs = P("fsdp", "group")
    return jax.shard_map(shards, mesh=mesh, in_specs=in_specs, out_specs=out_specs, check_vma=False)
```
